32 devices in a mesh: rep: 2 (over x), gx: 8 (over z, y), gy: 2 (over core).
Axes of the slice: x: 2, y: 2, z: 4, core: 2. Of those that a mesh axis runs over, the one named last changes fastest.
Arguments:
- tokens: bfloat16 [4, 128, 9216], P(None, ('rep', 'gx'), 'gy'), parts along dimension 1, may hold values from -6 to 6
- weight_in: bfloat16 [9216, 4096], P('gy', 'gx'), may hold values from -0.0625 to 0.0625
- weight_out: bfloat16 [4096, 9216], P('gx', 'gy'), may hold values from -0.09375 to 0.09375
Outputs:
- outputs: bfloat16 [4, 128, 9216], P(None, ('rep', 'gx'), 'gy'), parts along dimension 1
The draws below stay inside these ranges and needn't reach their ends.
There are 2 independent parts, one for each index of `rep`. The reference program is written for one: setup_inputs(seed, part) draws one part's arguments, and reference() takes and returns one part's arrays. A program takes and returns all parts, laid end to end along the dimension named above; an argument that names none is the same for every part. Nothing has to cross between parts.
All inputs are finite; a program needn't handle non-finite values.
Results may differ from the reference program's by a relative error of at most 0.023.
Values may be sent and summed in bfloat16 or wider, within the bound.
A program may use at most 64 MiB of HBM per device.

```python
import jax
import jax.numpy as jnp
from jax import lax

D = 9216
FF_DEV = 512
STEPS = 4
ROWS = 64
FF = 4096
N_GX = 8


def steps_of(key, extent, split, smallest, top_value):
    def one(position, shards_of):
        steps = jax.random.uniform(jax.random.fold_in(jax.random.fold_in(key, 6), position), (shards_of,), jnp.float32, smallest / len(split), top_value / len(split))
        return jnp.repeat(jnp.exp(steps), extent[position] // shards_of).reshape((-1,) + (1,) * (len(extent) - position - 1))

    level = one(*split[0])
    for cut in split[1:]:
        level = level * one(*cut)
    return level


def centred(own_key, dims, spread, most, shards=(), kind=jnp.bfloat16):
    entries = spread * jax.random.normal(own_key, dims, jnp.float32)
    if shards:
        entries = entries * steps_of(own_key, dims, shards, -0.22, 0.18)
    return jnp.clip(entries, -most, most).astype(kind)


def setup_inputs(seed: int = 0, part: int = 0) -> dict:
    arg_keys = jax.random.split(jax.random.key(seed), 4)
    part_keys = jax.random.split(jax.random.fold_in(arg_keys[3], part), 4)
    return {
        "tokens": centred(part_keys[0], (STEPS, ROWS, D), 1.0, 6.0, ((1, 8), (2, 2))),
        "weight_in": centred(arg_keys[1], (D, FF), D ** -0.5, 0.0625, ((0, 2), (1, 8))),
        "weight_out": centred(arg_keys[2], (FF, D), FF ** -0.5, 0.09375, ((0, 8), (1, 2))),
    }


def reference(tokens, weight_in, weight_out):
    results = []
    previous = None
    for step in range(STEPS):
        if previous is None:
            inputs = tokens[step]
        else:
            inputs = (tokens[step].astype(jnp.float32) + previous.astype(jnp.float32)).astype(jnp.bfloat16)
        pre = jnp.dot(inputs, weight_in, preferred_element_type=jnp.float32)
        hidden = jax.nn.gelu(pre, approximate=False).astype(jnp.bfloat16)

        def add_block(index, total):
            offset = (index * FF_DEV).astype(jnp.int32)
            cols = lax.dynamic_slice_in_dim(hidden, offset, FF_DEV, 1)
            rows = lax.dynamic_slice_in_dim(weight_out, offset, FF_DEV, 0)
            term = jnp.dot(cols, rows, preferred_element_type=jnp.float32).astype(jnp.bfloat16)
            return total + term.astype(jnp.float32)

        total = lax.fori_loop(jnp.int32(0), jnp.int32(N_GX), add_block, jnp.zeros((ROWS, D), jnp.float32))
        previous = total.astype(jnp.bfloat16)
        results.append(previous)
    return jnp.stack(results, 0)
```

```python
import functools

import jax
import jax.numpy as jnp
from jax import lax
from jax.experimental import pallas as pl
from jax.experimental.pallas import tpu as pltpu
from jax.sharding import PartitionSpec as P

MESH = pl.DeviceIdType.MESH
CHUNKS = 3
NEAR = 2


def gelu(x):
    return 0.5 * x * (1.0 + lax.erf(x * 0.7071067811865476))


def kernel(
    n, tok, w_in, w_out, out,
    win, wout, acc, hid, mine, xg, ps, pr, sy, ry, sz, rz,
    win_sem, wout_sem, agz_s, agz_r, agy_s, agy_r, p_s, p_r, rsy_s, rsy_r, rsz_s, rsz_r,
):
    steps, rows, d = tok.shape
    nz = n // NEAR
    width = d // CHUNKS
    gx = lax.axis_index("gx")
    gy = lax.axis_index("gy")
    y, z = lax.rem(gx, NEAR), lax.div(gx, NEAR)
    y_peer = {"gx": z * NEAR + (1 - y)}
    core_peer = {"gy": 1 - gy}

    def z_at(j):
        return lax.rem(z + j, nz)

    def z_id(zz):
        return {"gx": zz * NEAR + y}

    def cols(c):
        return pl.ds(c * width, width)

    def win_copy(c):
        return pltpu.make_async_copy(w_in.at[cols(c), :], win.at[cols(c), :], win_sem.at[c])

    def wout_copy(c):
        return pltpu.make_async_copy(w_out.at[:, cols(c)], wout.at[:, cols(c)], wout_sem.at[c])

    def remote(src, dst, s_sem, r_sem, to):
        return pltpu.make_async_remote_copy(
            src_ref=src, dst_ref=dst, send_sem=s_sem, recv_sem=r_sem, device_id=to, device_id_type=MESH
        )

    def ag_z(s, c, zz):
        return remote(xg.at[s, c, 0, z], xg.at[s, c, 0, z], agz_s.at[s, c, zz], agz_r.at[s, c, z], z_id(zz))

    def ag_z_in(s, c, zz):
        return remote(xg.at[s, c, 0, zz], xg.at[s, c, 0, zz], agz_s.at[s, c, zz], agz_r.at[s, c, zz], z_id(zz))

    def ag_y(s, c, zz):
        return remote(xg.at[s, c, 0, zz], xg.at[s, c, 1, zz], agy_s.at[s, c, zz], agy_r.at[s, c, zz], y_peer)

    def psum(s):
        return remote(ps.at[s], pr.at[s], p_s.at[s], p_r.at[s], core_peer)

    def rs_y(s, c):
        return remote(sy.at[s, c], ry.at[s, c], rsy_s.at[s, c], rsy_r.at[s, c], y_peer)

    def rs_z(s, c, zz):
        return remote(sz.at[s, c, zz], rz.at[s, c, z], rsz_s.at[s, c, zz], rsz_r.at[s, c, z], z_id(zz))

    def rs_z_in(s, c, zz):
        return remote(sz.at[s, c, zz], rz.at[s, c, zz], rsz_s.at[s, c, zz], rsz_r.at[s, c, zz], z_id(zz))

    for c in range(CHUNKS):
        win_copy(c).start()
    for c in range(CHUNKS):
        wout_copy(c).start()

    barrier = pltpu.get_barrier_semaphore()
    pl.semaphore_signal(barrier, inc=1, device_id=y_peer, device_id_type=MESH)
    pl.semaphore_signal(barrier, inc=1, device_id=core_peer, device_id_type=MESH)
    for j in range(1, nz):
        pl.semaphore_signal(barrier, inc=1, device_id=z_id(z_at(j)), device_id_type=MESH)
    pl.semaphore_wait(barrier, nz + 1)

    def send_inputs(s, c):
        ag_y(s, c, z).start()
        for j in range(1, nz):
            ag_z(s, c, z_at(j)).start()

    for c in range(CHUNKS):
        xg[0, c, 0, z] = tok[0, :, cols(c)]
        send_inputs(0, c)
    for c in range(CHUNKS):
        win_copy(c).wait()

    def step(s, carry):
        def project(c):
            for j in range(nz):
                ag_y(s, c, z_at(j)).wait_recv()
            part = jnp.dot(
                xg[s, c].reshape(n * rows, width), win[cols(c), :], preferred_element_type=jnp.float32
            )
            acc[...] = part if c == 0 else acc[...] + part

        for c in range(CHUNKS):
            for j in range(1, nz):
                zz = z_at(j)
                ag_z_in(s, c, zz).wait_recv()
                ag_y(s, c, zz).start()
            if c:
                project(c - 1)
        project(CHUNKS - 1)

        ps[s] = acc[...].astype(jnp.bfloat16)
        psum(s).start()

        @pl.when(s == 0)
        def _():
            for c in range(CHUNKS):
                wout_copy(c).wait()

        psum(s).wait_recv()
        hid[...] = gelu(acc[...] + pr[s].astype(jnp.float32)).astype(jnp.bfloat16)

        def pair_sum(c):
            rs_y(s, c).wait_recv()
            for j in range(1, nz):
                zz = z_at(j)
                sz[s, c, zz] = (mine[c, zz] + ry[s, c, zz].astype(jnp.float32)).astype(jnp.bfloat16)
                rs_z(s, c, zz).start()
            mine[c, z] = mine[c, z] + ry[s, c, z].astype(jnp.float32)

        for c in range(CHUNKS):
            terms = jnp.dot(hid[...], wout[:, cols(c)], preferred_element_type=jnp.float32)
            terms = terms.reshape(NEAR, nz, rows, width)
            sy[s, c] = terms[1].astype(jnp.bfloat16)
            rs_y(s, c).start()
            mine[c] = terms[0]
            if c:
                pair_sum(c - 1)
        pair_sum(CHUNKS - 1)

        for c in range(CHUNKS):
            total = mine[c, z]
            for j in range(1, nz):
                zz = z_at(j)
                rs_z_in(s, c, zz).wait_recv()
                total = total + rz[s, c, zz].astype(jnp.float32)
            result = total.astype(jnp.bfloat16)
            out[s, :, cols(c)] = result

            @pl.when(s < steps - 1)
            def _():
                nxt = tok[s + 1, :, cols(c)].astype(jnp.float32) + result.astype(jnp.float32)
                xg[s + 1, c, 0, z] = nxt.astype(jnp.bfloat16)
                send_inputs(s + 1, c)

        for c in range(CHUNKS):
            ag_y(s, c, z).wait_send()
            rs_y(s, c).wait_send()
            for j in range(1, nz):
                zz = z_at(j)
                ag_y(s, c, zz).wait_send()
                ag_z(s, c, zz).wait_send()
                rs_z(s, c, zz).wait_send()
        psum(s).wait_send()
        return carry

    lax.fori_loop(0, steps, step, 0)


def on_device(n, tokens, weight_in, weight_out):
    steps, rows, d = tokens.shape
    ff = weight_in.shape[1]
    nz = n // NEAR
    width = d // CHUNKS
    bf16, f32 = jnp.bfloat16, jnp.float32
    dma = pltpu.SemaphoreType.DMA
    flops = steps * n * rows * d * ff * 4
    return pl.pallas_call(
        functools.partial(kernel, n),
        out_shape=jax.ShapeDtypeStruct(tokens.shape, bf16),
        in_specs=[
            pl.BlockSpec(memory_space=pltpu.VMEM),
            pl.BlockSpec(memory_space=pl.ANY),
            pl.BlockSpec(memory_space=pl.ANY),
        ],
        out_specs=pl.BlockSpec(memory_space=pltpu.VMEM),
        scratch_shapes=[
            pltpu.VMEM((d, ff), bf16),
            pltpu.VMEM((ff, d), bf16),
            pltpu.VMEM((n * rows, ff), f32),
            pltpu.VMEM((n * rows, ff), bf16),
            pltpu.VMEM((CHUNKS, nz, rows, width), f32),
            pltpu.VMEM((steps, CHUNKS, NEAR, nz, rows, width), bf16),
            pltpu.VMEM((steps, n * rows, ff), bf16),
            pltpu.VMEM((steps, n * rows, ff), bf16),
            pltpu.VMEM((steps, CHUNKS, nz, rows, width), bf16),
            pltpu.VMEM((steps, CHUNKS, nz, rows, width), bf16),
            pltpu.VMEM((steps, CHUNKS, nz, rows, width), bf16),
            pltpu.VMEM((steps, CHUNKS, nz, rows, width), bf16),
            dma((CHUNKS,)),
            dma((CHUNKS,)),
            dma((steps, CHUNKS, nz)),
            dma((steps, CHUNKS, nz)),
            dma((steps, CHUNKS, nz)),
            dma((steps, CHUNKS, nz)),
            dma((steps,)),
            dma((steps,)),
            dma((steps, CHUNKS)),
            dma((steps, CHUNKS)),
            dma((steps, CHUNKS, nz)),
            dma((steps, CHUNKS, nz)),
        ],
        compiler_params=pltpu.CompilerParams(
            collective_id=0, has_side_effects=True, vmem_limit_bytes=60 * 1024 * 1024
        ),
        cost_estimate=pl.CostEstimate(
            flops=flops, bytes_accessed=4 * d * ff, transcendentals=steps * n * rows * ff
        ),
    )(tokens, weight_in, weight_out)


def solution(mesh):
    return jax.shard_map(
        functools.partial(on_device, mesh.shape["gx"]),
        mesh=mesh,
        in_specs=(P(None, ("rep", "gx"), "gy"), P("gy", "gx"), P("gx", "gy")),
        out_specs=P(None, ("rep", "gx"), "gy"),
        check_vma=False,
    )
```

```python
import functools

import jax
import jax.numpy as jnp
from jax import lax
from jax.experimental import pallas as pl
from jax.experimental.pallas import tpu as pltpu
from jax.sharding import PartitionSpec as P

MESH = pl.DeviceIdType.MESH
CHUNKS = 2
NEAR = 2


def gelu(x):
    return 0.5 * x * (1.0 + lax.erf(x * 0.7071067811865476))


def kernel(
    n, tok, w_in, w_out, out,
    win, wout, acc, hid, mine, xg, ps, pr, sy, ry, sz, rz,
    win_sem, wout_sem, agz_s, agz_r, agy_s, agy_r, p_s, p_r, rsy_s, rsy_r, rsz_s, rsz_r,
):
    steps, rows, d = tok.shape
    nz = n // NEAR
    width = d // CHUNKS
    gx = lax.axis_index("gx")
    gy = lax.axis_index("gy")
    y, z = lax.rem(gx, NEAR), lax.div(gx, NEAR)
    y_peer = {"gx": z * NEAR + (1 - y)}
    core_peer = {"gy": 1 - gy}

    def z_at(j):
        return lax.rem(z + j, nz)

    def z_id(zz):
        return {"gx": zz * NEAR + y}

    def cols(c):
        return pl.ds(c * width, width)

    def win_copy(c):
        return pltpu.make_async_copy(w_in.at[cols(c), :], win.at[cols(c), :], win_sem.at[c])

    def wout_copy(c):
        return pltpu.make_async_copy(w_out.at[:, cols(c)], wout.at[:, cols(c)], wout_sem.at[c])

    def remote(src, dst, s_sem, r_sem, to):
        return pltpu.make_async_remote_copy(
            src_ref=src, dst_ref=dst, send_sem=s_sem, recv_sem=r_sem, device_id=to, device_id_type=MESH
        )

    def ag_z(s, c, zz):
        return remote(xg.at[s, c, 0, z], xg.at[s, c, 0, z], agz_s.at[s, c, zz], agz_r.at[s, c, z], z_id(zz))

    def ag_z_in(s, c, zz):
        return remote(xg.at[s, c, 0, zz], xg.at[s, c, 0, zz], agz_s.at[s, c, zz], agz_r.at[s, c, zz], z_id(zz))

    def ag_y(s, c, zz):
        return remote(xg.at[s, c, 0, zz], xg.at[s, c, 1, zz], agy_s.at[s, c, zz], agy_r.at[s, c, zz], y_peer)

    def psum(s):
        return remote(ps.at[s], pr.at[s], p_s.at[s], p_r.at[s], core_peer)

    def rs_y(s, c, zz):
        return remote(sy.at[s, c, zz], ry.at[s, c, zz], rsy_s.at[s, c, zz], rsy_r.at[s, c, zz], y_peer)

    def rs_z(s, c, zz):
        return remote(sz.at[s, c, zz], rz.at[s, c, z], rsz_s.at[s, c, zz], rsz_r.at[s, c, z], z_id(zz))

    def rs_z_in(s, c, zz):
        return remote(sz.at[s, c, zz], rz.at[s, c, zz], rsz_s.at[s, c, zz], rsz_r.at[s, c, zz], z_id(zz))

    for c in range(CHUNKS):
        win_copy(c).start()
    for c in range(CHUNKS):
        wout_copy(c).start()

    barrier = pltpu.get_barrier_semaphore()
    pl.semaphore_signal(barrier, inc=1, device_id=y_peer, device_id_type=MESH)
    pl.semaphore_signal(barrier, inc=1, device_id=core_peer, device_id_type=MESH)
    for j in range(1, nz):
        pl.semaphore_signal(barrier, inc=1, device_id=z_id(z_at(j)), device_id_type=MESH)
    pl.semaphore_wait(barrier, nz + 1)

    def send_inputs(s, c):
        for j in range(nz - 1, 0, -1):
            ag_z(s, c, z_at(j)).start()
        ag_y(s, c, z).start()

    for c in range(CHUNKS):
        xg[0, c, 0, z] = tok[0, :, cols(c)]
        send_inputs(0, c)
    for c in range(CHUNKS):
        win_copy(c).wait()

    def step(s, carry):
        def project(c):
            for j in range(nz):
                ag_y(s, c, z_at(j)).wait_recv()
            part = jnp.dot(
                xg[s, c].reshape(n * rows, width), win[cols(c), :], preferred_element_type=jnp.float32
            )
            acc[...] = part if c == 0 else acc[...] + part

        for c in range(CHUNKS):
            for j in range(1, nz):
                zz = z_at(j)
                ag_z_in(s, c, zz).wait_recv()
                ag_y(s, c, zz).start()
            if c:
                project(c - 1)
        project(CHUNKS - 1)

        ps[s] = acc[...].astype(jnp.bfloat16)
        psum(s).start()

        @pl.when(s == 0)
        def _():
            for c in range(CHUNKS):
                wout_copy(c).wait()

        psum(s).wait_recv()
        hid[...] = gelu(acc[...] + pr[s].astype(jnp.float32)).astype(jnp.bfloat16)

        def pair_sum(c):
            for j in range(1, nz):
                zz = z_at(j)
                rs_y(s, c, zz).wait_recv()
                sz[s, c, zz] = (mine[c, zz] + ry[s, c, zz].astype(jnp.float32)).astype(jnp.bfloat16)
                rs_z(s, c, zz).start()
            rs_y(s, c, z).wait_recv()
            mine[c, z] = mine[c, z] + ry[s, c, z].astype(jnp.float32)

        for c in range(CHUNKS):
            terms = jnp.dot(hid[...], wout[:, cols(c)], preferred_element_type=jnp.float32)
            terms = terms.reshape(NEAR, nz, rows, width)
            sy[s, c] = terms[1].astype(jnp.bfloat16)
            for j in range(nz):
                rs_y(s, c, z_at((j + 1) % nz)).start()
            mine[c] = terms[0]
            if c:
                pair_sum(c - 1)
        pair_sum(CHUNKS - 1)

        for c in range(CHUNKS):
            total = mine[c, z]
            for j in range(1, nz):
                zz = z_at(j)
                rs_z_in(s, c, zz).wait_recv()
                total = total + rz[s, c, zz].astype(jnp.float32)
            result = total.astype(jnp.bfloat16)
            out[s, :, cols(c)] = result

            @pl.when(s < steps - 1)
            def _():
                nxt = tok[s + 1, :, cols(c)].astype(jnp.float32) + result.astype(jnp.float32)
                xg[s + 1, c, 0, z] = nxt.astype(jnp.bfloat16)
                send_inputs(s + 1, c)

        for c in range(CHUNKS):
            ag_y(s, c, z).wait_send()
            for zz in range(nz):
                rs_y(s, c, zz).wait_send()
            for j in range(1, nz):
                zz = z_at(j)
                ag_y(s, c, zz).wait_send()
                ag_z(s, c, zz).wait_send()
                rs_z(s, c, zz).wait_send()
        psum(s).wait_send()
        return carry

    lax.fori_loop(0, steps, step, 0)


def on_device(n, tokens, weight_in, weight_out):
    steps, rows, d = tokens.shape
    ff = weight_in.shape[1]
    nz = n // NEAR
    width = d // CHUNKS
    bf16, f32 = jnp.bfloat16, jnp.float32
    dma = pltpu.SemaphoreType.DMA
    flops = steps * n * rows * d * ff * 4
    return pl.pallas_call(
        functools.partial(kernel, n),
        out_shape=jax.ShapeDtypeStruct(tokens.shape, bf16),
        in_specs=[
            pl.BlockSpec(memory_space=pltpu.VMEM),
            pl.BlockSpec(memory_space=pl.ANY),
            pl.BlockSpec(memory_space=pl.ANY),
        ],
        out_specs=pl.BlockSpec(memory_space=pltpu.VMEM),
        scratch_shapes=[
            pltpu.VMEM((d, ff), bf16),
            pltpu.VMEM((ff, d), bf16),
            pltpu.VMEM((n * rows, ff), f32),
            pltpu.VMEM((n * rows, ff), bf16),
            pltpu.VMEM((CHUNKS, nz, rows, width), f32),
            pltpu.VMEM((steps, CHUNKS, NEAR, nz, rows, width), bf16),
            pltpu.VMEM((steps, n * rows, ff), bf16),
            pltpu.VMEM((steps, n * rows, ff), bf16),
            pltpu.VMEM((steps, CHUNKS, nz, rows, width), bf16),
            pltpu.VMEM((steps, CHUNKS, nz, rows, width), bf16),
            pltpu.VMEM((steps, CHUNKS, nz, rows, width), bf16),
            pltpu.VMEM((steps, CHUNKS, nz, rows, width), bf16),
            dma((CHUNKS,)),
            dma((CHUNKS,)),
            dma((steps, CHUNKS, nz)),
            dma((steps, CHUNKS, nz)),
            dma((steps, CHUNKS, nz)),
            dma((steps, CHUNKS, nz)),
            dma((steps,)),
            dma((steps,)),
            dma((steps, CHUNKS, nz)),
            dma((steps, CHUNKS, nz)),
            dma((steps, CHUNKS, nz)),
            dma((steps, CHUNKS, nz)),
        ],
        compiler_params=pltpu.CompilerParams(
            collective_id=0, has_side_effects=True, vmem_limit_bytes=60 * 1024 * 1024
        ),
        cost_estimate=pl.CostEstimate(
            flops=flops, bytes_accessed=4 * d * ff, transcendentals=steps * n * rows * ff
        ),
    )(tokens, weight_in, weight_out)


def solution(mesh):
    return jax.shard_map(
        functools.partial(on_device, mesh.shape["gx"]),
        mesh=mesh,
        in_specs=(P(None, ("rep", "gx"), "gy"), P("gy", "gx"), P("gx", "gy")),
        out_specs=P(None, ("rep", "gx"), "gy"),
        check_vma=False,
    )
```

```python
import functools

import jax
import jax.numpy as jnp
from jax import lax
from jax.experimental import pallas as pl
from jax.experimental.pallas import tpu as pltpu
from jax.sharding import PartitionSpec as P

MESH = pl.DeviceIdType.MESH
CHUNKS = 2
NEAR = 2


def gelu(x):
    return 0.5 * x * (1.0 + lax.erf(x * 0.7071067811865476))


def kernel(
    n, tok, w_in, w_out, out,
    win, wout, acc, hid, mine, xg, ps, pr, sy, ry, sz, rz,
    win_sem, wout_sem, agz_s, agz_r, agy_s, agy_r, p_s, p_r, rsy_s, rsy_r, rsz_s, rsz_r,
):
    steps, rows, d = tok.shape
    nz = n // NEAR
    width = d // CHUNKS
    gx = lax.axis_index("gx")
    gy = lax.axis_index("gy")
    y, z = lax.rem(gx, NEAR), lax.div(gx, NEAR)
    y_peer = {"gx": z * NEAR + (1 - y)}
    core_peer = {"gy": 1 - gy}

    toward = jnp.where(z < nz // 2, 1, -1)
    margin = jnp.minimum(z, nz - 1 - z)

    mate = z + 1 - 2 * lax.rem(z, 2)

    def z_at(j):
        near = toward * ((j + 1) // 2) * (1 if j % 2 else -1)
        return z + jnp.where(j <= 2 * margin, near, toward * (j - margin))

    def z_id(zz):
        return {"gx": zz * NEAR + y}

    def cols(c):
        return pl.ds(c * width, width)

    def win_copy(c):
        return pltpu.make_async_copy(w_in.at[cols(c), :], win.at[cols(c), :], win_sem.at[c])

    def wout_copy(c):
        return pltpu.make_async_copy(w_out.at[:, cols(c)], wout.at[:, cols(c)], wout_sem.at[c])

    def remote(src, dst, s_sem, r_sem, to):
        return pltpu.make_async_remote_copy(
            src_ref=src, dst_ref=dst, send_sem=s_sem, recv_sem=r_sem, device_id=to, device_id_type=MESH
        )

    def ag_z(s, c, zz):
        return remote(xg.at[s, c, 0, z], xg.at[s, c, 0, z], agz_s.at[s, c, zz], agz_r.at[s, c, z], z_id(zz))

    def ag_z_in(s, c, zz):
        return remote(xg.at[s, c, 0, zz], xg.at[s, c, 0, zz], agz_s.at[s, c, zz], agz_r.at[s, c, zz], z_id(zz))

    def ag_y(s, c, zz):
        return remote(xg.at[s, c, 0, zz], xg.at[s, c, 1, zz], agy_s.at[s, c, zz], agy_r.at[s, c, zz], y_peer)

    def ag_cross(s, c, zz):
        to = {"gx": zz * NEAR + (1 - y)}
        return remote(xg.at[s, c, 0, z], xg.at[s, c, 1, z], agy_s.at[s, c, zz], agy_r.at[s, c, z], to)

    def psum(s):
        return remote(ps.at[s], pr.at[s], p_s.at[s], p_r.at[s], core_peer)

    def rs_y(s, c, zz):
        return remote(sy.at[s, c, zz], ry.at[s, c, zz], rsy_s.at[s, c, zz], rsy_r.at[s, c, zz], y_peer)

    def rs_z(s, c, zz):
        return remote(sz.at[s, c, zz], rz.at[s, c, z], rsz_s.at[s, c, zz], rsz_r.at[s, c, z], z_id(zz))

    def rs_z_in(s, c, zz):
        return remote(sz.at[s, c, zz], rz.at[s, c, zz], rsz_s.at[s, c, zz], rsz_r.at[s, c, zz], z_id(zz))

    for c in range(CHUNKS):
        win_copy(c).start()
    for c in range(CHUNKS):
        wout_copy(c).start()

    barrier = pltpu.get_barrier_semaphore()
    pl.semaphore_signal(barrier, inc=1, device_id=y_peer, device_id_type=MESH)
    pl.semaphore_signal(barrier, inc=1, device_id=core_peer, device_id_type=MESH)
    for j in range(1, nz):
        pl.semaphore_signal(barrier, inc=1, device_id=z_id(z_at(j)), device_id_type=MESH)
    cross = {"gx": mate * NEAR + (1 - y)}
    pl.semaphore_signal(barrier, inc=1, device_id=cross, device_id_type=MESH)
    pl.semaphore_wait(barrier, nz + 2)

    def send_inputs(s, c):
        for j in range(1, nz):
            ag_z(s, c, z_at(j)).start()
        ag_y(s, c, z).start()
        ag_cross(s, c, mate).start()

    for c in range(CHUNKS):
        xg[0, c, 0, z] = tok[0, :, cols(c)]
        send_inputs(0, c)
    def step(s, carry):
        def project(c):
            @pl.when(s == 0)
            def _():
                win_copy(c).wait()

            for j in range(nz):
                ag_y(s, c, z_at(j)).wait_recv()
            part = jnp.dot(
                xg[s, c].reshape(n * rows, width), win[cols(c), :], preferred_element_type=jnp.float32
            )
            acc[...] = part if c == 0 else acc[...] + part

        for c in range(CHUNKS):
            for j in range(1, nz):
                zz = z_at(j)
                ag_z_in(s, c, zz).wait_recv()

                @pl.when(zz != mate)
                def _():
                    ag_y(s, c, zz).start()

            if c:
                project(c - 1)
        project(CHUNKS - 1)

        ps[s] = acc[...].astype(jnp.bfloat16)
        psum(s).start()

        @pl.when(s == 0)
        def _():
            for c in range(CHUNKS):
                wout_copy(c).wait()

        psum(s).wait_recv()
        hid[...] = gelu(acc[...] + pr[s].astype(jnp.float32)).astype(jnp.bfloat16)

        def pair_sum(c):
            for j in range(nz - 1, 0, -1):
                zz = z_at(j)
                rs_y(s, c, zz).wait_recv()
                sz[s, c, zz] = (mine[c, zz] + ry[s, c, zz].astype(jnp.float32)).astype(jnp.bfloat16)
                rs_z(s, c, zz).start()
            rs_y(s, c, z).wait_recv()
            mine[c, z] = mine[c, z] + ry[s, c, z].astype(jnp.float32)

        for c in range(CHUNKS):
            terms = jnp.dot(hid[...], wout[:, cols(c)], preferred_element_type=jnp.float32)
            terms = terms.reshape(NEAR, nz, rows, width)
            sy[s, c] = terms[1].astype(jnp.bfloat16)
            for j in range(nz - 1, -1, -1):
                rs_y(s, c, z_at(j)).start()
            mine[c] = terms[0]
            if c:
                pair_sum(c - 1)
        pair_sum(CHUNKS - 1)

        for c in range(CHUNKS):
            total = mine[c, z]
            for j in range(1, nz):
                zz = z_at(j)
                rs_z_in(s, c, zz).wait_recv()
                total = total + rz[s, c, zz].astype(jnp.float32)
            result = total.astype(jnp.bfloat16)
            out[s, :, cols(c)] = result

            @pl.when(s < steps - 1)
            def _():
                nxt = tok[s + 1, :, cols(c)].astype(jnp.float32) + result.astype(jnp.float32)
                xg[s + 1, c, 0, z] = nxt.astype(jnp.bfloat16)
                send_inputs(s + 1, c)

        for c in range(CHUNKS):
            ag_y(s, c, z).wait_send()
            for zz in range(nz):
                rs_y(s, c, zz).wait_send()
            for j in range(1, nz):
                zz = z_at(j)
                ag_y(s, c, zz).wait_send()
                ag_z(s, c, zz).wait_send()
                rs_z(s, c, zz).wait_send()
        psum(s).wait_send()
        return carry

    lax.fori_loop(0, steps, step, 0)


def on_device(n, tokens, weight_in, weight_out):
    steps, rows, d = tokens.shape
    ff = weight_in.shape[1]
    nz = n // NEAR
    width = d // CHUNKS
    bf16, f32 = jnp.bfloat16, jnp.float32
    dma = pltpu.SemaphoreType.DMA
    flops = steps * n * rows * d * ff * 4
    return pl.pallas_call(
        functools.partial(kernel, n),
        out_shape=jax.ShapeDtypeStruct(tokens.shape, bf16),
        in_specs=[
            pl.BlockSpec(memory_space=pltpu.VMEM),
            pl.BlockSpec(memory_space=pl.ANY),
            pl.BlockSpec(memory_space=pl.ANY),
        ],
        out_specs=pl.BlockSpec(memory_space=pltpu.VMEM),
        scratch_shapes=[
            pltpu.VMEM((d, ff), bf16),
            pltpu.VMEM((ff, d), bf16),
            pltpu.VMEM((n * rows, ff), f32),
            pltpu.VMEM((n * rows, ff), bf16),
            pltpu.VMEM((CHUNKS, nz, rows, width), f32),
            pltpu.VMEM((steps, CHUNKS, NEAR, nz, rows, width), bf16),
            pltpu.VMEM((steps, n * rows, ff), bf16),
            pltpu.VMEM((steps, n * rows, ff), bf16),
            pltpu.VMEM((steps, CHUNKS, nz, rows, width), bf16),
            pltpu.VMEM((steps, CHUNKS, nz, rows, width), bf16),
            pltpu.VMEM((steps, CHUNKS, nz, rows, width), bf16),
            pltpu.VMEM((steps, CHUNKS, nz, rows, width), bf16),
            dma((CHUNKS,)),
            dma((CHUNKS,)),
            dma((steps, CHUNKS, nz)),
            dma((steps, CHUNKS, nz)),
            dma((steps, CHUNKS, nz)),
            dma((steps, CHUNKS, nz)),
            dma((steps,)),
            dma((steps,)),
            dma((steps, CHUNKS, nz)),
            dma((steps, CHUNKS, nz)),
            dma((steps, CHUNKS, nz)),
            dma((steps, CHUNKS, nz)),
        ],
        compiler_params=pltpu.CompilerParams(
            collective_id=0, has_side_effects=True, vmem_limit_bytes=60 * 1024 * 1024
        ),
        cost_estimate=pl.CostEstimate(
            flops=flops, bytes_accessed=4 * d * ff, transcendentals=steps * n * rows * ff
        ),
    )(tokens, weight_in, weight_out)


def solution(mesh):
    return jax.shard_map(
        functools.partial(on_device, mesh.shape["gx"]),
        mesh=mesh,
        in_specs=(P(None, ("rep", "gx"), "gy"), P("gy", "gx"), P("gx", "gy")),
        out_specs=P(None, ("rep", "gx"), "gy"),
        check_vma=False,
    )
```

```python
import functools

import jax
import jax.numpy as jnp
from jax import lax
from jax.experimental import pallas as pl
from jax.experimental.pallas import tpu as pltpu
from jax.sharding import PartitionSpec as P

MESH = pl.DeviceIdType.MESH
CHUNKS = 2
NEAR = 2


def gelu(x):
    return 0.5 * x * (1.0 + lax.erf(x * 0.7071067811865476))


def kernel(
    n, tok, w_in, w_out, out,
    win, wout, acc, hid, mine, xg, ps, pr, sy, ry, sz, rz,
    win_sem, wout_sem, agz_s, agz_r, agy_s, agy_r, p_s, p_r, rsy_s, rsy_r, rsz_s, rsz_r,
):
    steps, rows, d = tok.shape
    nz = n // NEAR
    width = d // CHUNKS
    gx = lax.axis_index("gx")
    gy = lax.axis_index("gy")
    y, z = lax.rem(gx, NEAR), lax.div(gx, NEAR)
    y_peer = {"gx": z * NEAR + (1 - y)}
    core_peer = {"gy": 1 - gy}

    toward = jnp.where(z < nz // 2, 1, -1)
    margin = jnp.minimum(z, nz - 1 - z)

    mate = z + 1 - 2 * lax.rem(z, 2)

    def z_at(j):
        near = toward * ((j + 1) // 2) * (1 if j % 2 else -1)
        return z + jnp.where(j <= 2 * margin, near, toward * (j - margin))

    def z_id(zz):
        return {"gx": zz * NEAR + y}

    def cols(c):
        return pl.ds(c * width, width)

    def win_copy(c):
        return pltpu.make_async_copy(w_in.at[cols(c), :], win.at[cols(c), :], win_sem.at[c])

    def wout_copy(c):
        return pltpu.make_async_copy(w_out.at[:, cols(c)], wout.at[:, cols(c)], wout_sem.at[c])

    def remote(src, dst, s_sem, r_sem, to):
        return pltpu.make_async_remote_copy(
            src_ref=src, dst_ref=dst, send_sem=s_sem, recv_sem=r_sem, device_id=to, device_id_type=MESH
        )

    def ag_z(s, c, zz):
        return remote(xg.at[s, c, 0, z], xg.at[s, c, 0, z], agz_s.at[s, c, zz], agz_r.at[s, c, z], z_id(zz))

    def ag_z_in(s, c, zz):
        return remote(xg.at[s, c, 0, zz], xg.at[s, c, 0, zz], agz_s.at[s, c, zz], agz_r.at[s, c, zz], z_id(zz))

    def ag_y(s, c, zz):
        return remote(xg.at[s, c, 0, zz], xg.at[s, c, 1, zz], agy_s.at[s, c, zz], agy_r.at[s, c, zz], y_peer)

    def ag_cross(s, c, zz):
        to = {"gx": zz * NEAR + (1 - y)}
        return remote(xg.at[s, c, 0, z], xg.at[s, c, 1, z], agy_s.at[s, c, zz], agy_r.at[s, c, z], to)

    def psum(s):
        return remote(ps.at[s], pr.at[s], p_s.at[s], p_r.at[s], core_peer)

    def rs_y(s, c, zz):
        return remote(sy.at[s, c, zz], ry.at[s, c, zz], rsy_s.at[s, c, zz], rsy_r.at[s, c, zz], y_peer)

    def rs_z(s, c, zz):
        return remote(sz.at[s, c, zz], rz.at[s, c, z], rsz_s.at[s, c, zz], rsz_r.at[s, c, z], z_id(zz))

    def rs_z_in(s, c, zz):
        return remote(sz.at[s, c, zz], rz.at[s, c, zz], rsz_s.at[s, c, zz], rsz_r.at[s, c, zz], z_id(zz))

    for c in range(CHUNKS):
        win_copy(c).start()
    for c in range(CHUNKS):
        wout_copy(c).start()

    barrier = pltpu.get_barrier_semaphore()
    pl.semaphore_signal(barrier, inc=1, device_id=y_peer, device_id_type=MESH)
    pl.semaphore_signal(barrier, inc=1, device_id=core_peer, device_id_type=MESH)
    for j in range(1, nz):
        pl.semaphore_signal(barrier, inc=1, device_id=z_id(z_at(j)), device_id_type=MESH)
    cross = {"gx": mate * NEAR + (1 - y)}
    pl.semaphore_signal(barrier, inc=1, device_id=cross, device_id_type=MESH)
    pl.semaphore_wait(barrier, nz + 2)

    def send_inputs(s, c):
        for j in range(1, nz):
            ag_z(s, c, z_at(j)).start()
        ag_y(s, c, z).start()
        ag_cross(s, c, mate).start()

    for c in range(CHUNKS):
        xg[0, c, 0, z] = tok[0, :, cols(c)]
        send_inputs(0, c)
    def step(s, carry):
        def project(c):
            @pl.when(s == 0)
            def _():
                win_copy(c).wait()

            for j in range(nz):
                ag_y(s, c, z_at(j)).wait_recv()
            part = jnp.dot(
                xg[s, c].reshape(n * rows, width), win[cols(c), :], preferred_element_type=jnp.float32
            )
            acc[...] = part if c == 0 else acc[...] + part

        for c in range(CHUNKS):
            for j in range(1, nz):
                zz = z_at(j)
                ag_z_in(s, c, zz).wait_recv()

                @pl.when(zz != mate)
                def _():
                    ag_y(s, c, zz).start()

            if c:
                project(c - 1)
        project(CHUNKS - 1)

        ps[s] = acc[...].astype(jnp.bfloat16)
        psum(s).start()

        @pl.when(s == 0)
        def _():
            for c in range(CHUNKS):
                wout_copy(c).wait()

        psum(s).wait_recv()
        hid[...] = gelu(acc[...] + pr[s].astype(jnp.float32)).astype(jnp.bfloat16)

        def pair_sum(c):
            for j in range(nz - 1, 0, -1):
                zz = z_at(j)
                rs_y(s, c, zz).wait_recv()
                sz[s, c, zz] = (mine[c, zz] + ry[s, c, zz].astype(jnp.float32)).astype(jnp.bfloat16)
                rs_z(s, c, zz).start()

        for c in range(CHUNKS):
            terms = jnp.dot(hid[...], wout[:, cols(c)], preferred_element_type=jnp.float32)
            terms = terms.reshape(NEAR, nz, rows, width)
            sy[s, c] = terms[1].astype(jnp.bfloat16)
            for j in range(nz - 1, -1, -1):
                rs_y(s, c, z_at(j)).start()
            mine[c] = terms[0]
            if c:
                pair_sum(c - 1)
        pair_sum(CHUNKS - 1)

        for c in range(CHUNKS):
            rs_y(s, c, z).wait_recv()
            total = mine[c, z] + ry[s, c, z].astype(jnp.float32)
            for j in range(1, nz):
                zz = z_at(j)
                rs_z_in(s, c, zz).wait_recv()
                total = total + rz[s, c, zz].astype(jnp.float32)
            result = total.astype(jnp.bfloat16)
            out[s, :, cols(c)] = result

            @pl.when(s < steps - 1)
            def _():
                nxt = tok[s + 1, :, cols(c)].astype(jnp.float32) + result.astype(jnp.float32)
                xg[s + 1, c, 0, z] = nxt.astype(jnp.bfloat16)
                send_inputs(s + 1, c)

        for c in range(CHUNKS):
            ag_y(s, c, z).wait_send()
            for zz in range(nz):
                rs_y(s, c, zz).wait_send()
            for j in range(1, nz):
                zz = z_at(j)
                ag_y(s, c, zz).wait_send()
                ag_z(s, c, zz).wait_send()
                rs_z(s, c, zz).wait_send()
        psum(s).wait_send()
        return carry

    lax.fori_loop(0, steps, step, 0)


def on_device(n, tokens, weight_in, weight_out):
    steps, rows, d = tokens.shape
    ff = weight_in.shape[1]
    nz = n // NEAR
    width = d // CHUNKS
    bf16, f32 = jnp.bfloat16, jnp.float32
    dma = pltpu.SemaphoreType.DMA
    flops = steps * n * rows * d * ff * 4
    return pl.pallas_call(
        functools.partial(kernel, n),
        out_shape=jax.ShapeDtypeStruct(tokens.shape, bf16),
        in_specs=[
            pl.BlockSpec(memory_space=pltpu.VMEM),
            pl.BlockSpec(memory_space=pl.ANY),
            pl.BlockSpec(memory_space=pl.ANY),
        ],
        out_specs=pl.BlockSpec(memory_space=pltpu.VMEM),
        scratch_shapes=[
            pltpu.VMEM((d, ff), bf16),
            pltpu.VMEM((ff, d), bf16),
            pltpu.VMEM((n * rows, ff), f32),
            pltpu.VMEM((n * rows, ff), bf16),
            pltpu.VMEM((CHUNKS, nz, rows, width), f32),
            pltpu.VMEM((steps, CHUNKS, NEAR, nz, rows, width), bf16),
            pltpu.VMEM((steps, n * rows, ff), bf16),
            pltpu.VMEM((steps, n * rows, ff), bf16),
            pltpu.VMEM((steps, CHUNKS, nz, rows, width), bf16),
            pltpu.VMEM((steps, CHUNKS, nz, rows, width), bf16),
            pltpu.VMEM((steps, CHUNKS, nz, rows, width), bf16),
            pltpu.VMEM((steps, CHUNKS, nz, rows, width), bf16),
            dma((CHUNKS,)),
            dma((CHUNKS,)),
            dma((steps, CHUNKS, nz)),
            dma((steps, CHUNKS, nz)),
            dma((steps, CHUNKS, nz)),
            dma((steps, CHUNKS, nz)),
            dma((steps,)),
            dma((steps,)),
            dma((steps, CHUNKS, nz)),
            dma((steps, CHUNKS, nz)),
            dma((steps, CHUNKS, nz)),
            dma((steps, CHUNKS, nz)),
        ],
        compiler_params=pltpu.CompilerParams(
            collective_id=0, has_side_effects=True, vmem_limit_bytes=60 * 1024 * 1024
        ),
        cost_estimate=pl.CostEstimate(
            flops=flops, bytes_accessed=4 * d * ff, transcendentals=steps * n * rows * ff
        ),
    )(tokens, weight_in, weight_out)


def solution(mesh):
    return jax.shard_map(
        functools.partial(on_device, mesh.shape["gx"]),
        mesh=mesh,
        in_specs=(P(None, ("rep", "gx"), "gy"), P("gy", "gx"), P("gx", "gy")),
        out_specs=P(None, ("rep", "gx"), "gy"),
        check_vma=False,
    )
```
